512 devices in a mesh: depth: 8 (over x, z_hi), row: 4 (over y), col: 16 (over z_lo, core).
Axes of the slice: x: 4, y: 4, z: 16 (z_hi: 2, z_lo: 8; z = z_hi * 8 + z_lo), core: 2. Of those that a mesh axis runs over, the one named last changes fastest.
Arguments:
- x_out: float32 [8192, 768], P(('depth', 'col'), 'row'), may hold values from -6 to 6
- v_out: float32 [8192, 768], P(('depth', 'col'), 'row'), may hold values from -6 to 6
- dx_out: float32 [8192, 768], P(('depth', 'col'), 'row'), may hold values from -6 to 6
- dv_out: float32 [8192, 768], P(('depth', 'col'), 'row'), may hold values from -6 to 6
- gate_weight: bfloat16 [14336, 8192], P(('col', 'row'), 'depth'), may hold values from -0.0625 to 0.0625
- up_weight: bfloat16 [14336, 8192], P(('col', 'row'), 'depth'), may hold values from -0.0625 to 0.0625
- down_weight: bfloat16 [14336, 8192], P(('col', 'row'), 'depth'), may hold values from -0.046875 to 0.046875
Outputs:
- x_prev: float32 [8192, 768], P(('depth', 'col'), 'row')
- v_prev: float32 [8192, 768], P(('depth', 'col'), 'row')
- dx_prev: float32 [8192, 768], P(('depth', 'col'), 'row')
- grad_gate: float32 [14336, 8192], P(('col', 'row'), 'depth')
- grad_up: float32 [14336, 8192], P(('col', 'row'), 'depth')
- grad_down: float32 [14336, 8192], P(('col', 'row'), 'depth')
The draws below stay inside these ranges and needn't reach their ends.
All inputs are finite; a program needn't handle non-finite values.
Results may differ from the reference program's by a relative error of at most 0.0061.
Values may be sent and summed in bfloat16 or wider, within the bound.
No kernel may reach another device: no remote copies, remote signals or barrier semaphores. Data moves between devices by JAX's collectives and lax.ppermute only.
A program may use at most 64 MiB of HBM per device.

```python
import jax
import jax.numpy as jnp

D = 8192
FF = 14336
TOKENS = 768


def block_scale(rng, dims, pieces, low, largest):
    def one(position, shards_of):
        steps = jax.random.uniform(jax.random.fold_in(jax.random.fold_in(rng, 6), position), (shards_of,), jnp.float32, low / len(pieces), largest / len(pieces))
        return jnp.repeat(jnp.exp(steps), dims[position] // shards_of).reshape((-1,) + (1,) * (len(dims) - position - 1))

    loudness = one(*pieces[0])
    for cut in pieces[1:]:
        loudness = loudness * one(*cut)
    return loudness


def bell_draw(key, dims, deviation, most, cuts=(), dtype=jnp.bfloat16):
    loudness = block_scale(key, dims, cuts, -0.22, 0.18) if cuts else 1.0
    entries = jax.random.normal(key, dims, jnp.float32) * deviation * loudness
    return jnp.minimum(jnp.maximum(entries, -most), most).astype(dtype)


def setup_inputs(seed: int = 0) -> dict:
    arg_keys = jax.random.split(jax.random.key(seed), 8)
    return {
        "x_out": bell_draw(arg_keys[0], (D, TOKENS), 1.0, 6.0, ((0, 128), (1, 4)), jnp.float32),
        "v_out": bell_draw(arg_keys[1], (D, TOKENS), 1.0, 6.0, ((0, 128), (1, 4)), jnp.float32),
        "dx_out": bell_draw(arg_keys[2], (D, TOKENS), 1.0, 6.0, ((0, 128), (1, 4)), jnp.float32),
        "dv_out": bell_draw(arg_keys[3], (D, TOKENS), 1.0, 6.0, ((0, 128), (1, 4)), jnp.float32),
        "gate_weight": bell_draw(arg_keys[4], (FF, D), D ** -0.5, 0.0625, ((0, 64), (1, 8))),
        "up_weight": bell_draw(arg_keys[5], (FF, D), D ** -0.5, 0.0625, ((0, 64), (1, 8))),
        "down_weight": bell_draw(arg_keys[6], (FF, D), FF ** -0.5, 0.046875, ((0, 64), (1, 8))),
    }


momentum = 0.5


def mult(left, right):
    return jnp.dot(left.astype(jnp.float32), right.astype(jnp.float32), preferred_element_type=jnp.float32)


def reference(x_out, v_out, dx_out, dv_out, gate_weight, up_weight, down_weight):
    x_prev = x_out - v_out
    x_half = x_prev.astype(jnp.bfloat16)
    df = ((1.0 - momentum) * (dx_out + dv_out)).astype(jnp.bfloat16)
    gate = mult(gate_weight, x_half)
    up = mult(up_weight, x_half)
    sig = jax.nn.sigmoid(gate)
    act = (gate * sig * up).astype(jnp.bfloat16)
    y_out = mult(down_weight.T, act)
    v_prev = (v_out - (1.0 - momentum) * y_out) / momentum
    d_act = mult(down_weight, df)
    d_gate = (d_act * up * sig * (1.0 + gate * (1.0 - sig))).astype(jnp.bfloat16)
    d_up = (d_act * gate * sig).astype(jnp.bfloat16)
    dx_prev = dx_out + (mult(gate_weight.T, d_gate) + mult(up_weight.T, d_up))
    grad_gate = mult(d_gate, x_half.T)
    grad_up = mult(d_up, x_half.T)
    grad_down = mult(act, df.T)
    return (x_prev, v_prev, dx_prev, grad_gate, grad_up, grad_down)
```

```python
import jax
import jax.numpy as jnp
from jax import lax
from jax.sharding import PartitionSpec as P

momentum = 0.5
BF = jnp.bfloat16
F32 = jnp.float32


def copies(block, count):
    return jnp.broadcast_to(block[None], (count,) + block.shape)


def nonlinear(gate, up_val, d_act):
    sig = jax.nn.sigmoid(gate)
    act = (gate * sig * up_val).astype(BF)
    d_gate = (d_act * up_val * sig * (1.0 + gate * (1.0 - sig))).astype(BF)
    d_up = (d_act * gate * sig).astype(BF)
    return jnp.stack([act, d_gate, d_up])


def make(depth, rows, cols):
    count_x, count_z = depth // 2, cols // 2
    x_groups = [[2 * x + h for x in range(count_x)] for h in range(2)]
    z_groups = [[2 * z + k for z in range(count_z)] for k in range(2)]
    swap_core = [(c, c ^ 1) for c in range(cols)]
    swap_half = [(d, d ^ 1) for d in range(depth)]

    def over_x(blocks):
        return lax.all_to_all(blocks, "depth", 0, 0, axis_index_groups=x_groups)

    def over_z(blocks):
        return lax.all_to_all(blocks, "col", 0, 0, axis_index_groups=z_groups)

    def over_row(blocks):
        return lax.all_to_all(blocks, "row", 0, 0)

    def other_core(block):
        return lax.ppermute(block, "col", swap_core)

    def on_device(x_out, v_out, dx_out, dv_out, gate_weight, up_weight, down_weight):
        feats, toks = x_out.shape
        half = toks // 2
        hid = gate_weight.shape[0]
        core = lax.axis_index("col") % 2
        first = core == 0

        gate_w = jnp.concatenate([gate_weight, other_core(gate_weight)])
        up_w = jnp.concatenate([up_weight, other_core(up_weight)])
        down_w = jnp.concatenate([down_weight, other_core(down_weight)])

        x_prev = x_out - v_out
        x_half = x_prev.astype(BF)
        df_half = ((1.0 - momentum) * (dx_out + dv_out)).astype(BF)
        both = jnp.stack([x_half.T, df_half.T]).reshape(2, 2, half, feats)
        mine = jnp.where(first, both[:, 0], both[:, 1])
        theirs = other_core(jnp.where(first, both[:, 1], both[:, 0]))
        block = jnp.where(
            first, jnp.concatenate([mine, theirs], -1), jnp.concatenate([theirs, mine], -1)
        )

        along_z = over_z(copies(block, count_z))
        inputs = over_row(copies(along_z, rows))
        other_inputs = other_core(inputs)

        def forward(weight, which):
            return jnp.einsum(
                "hzf,rztf->hrt",
                weight.reshape(2 * hid, count_z, 2 * feats),
                inputs[:, :, which],
                preferred_element_type=F32,
            ).reshape(count_x, 2 * hid // count_x, rows * half)

        parts = jnp.stack(
            [forward(gate_w, 0), forward(up_w, 0), forward(down_w, 1)], 1
        ).astype(BF)
        sums = over_x(parts).astype(F32).sum(0)
        sums = sums + lax.ppermute(sums.astype(BF), "depth", swap_half).astype(F32)
        hidden = over_x(copies(nonlinear(sums[0], sums[1], sums[2]), count_x))
        hidden = jnp.swapaxes(hidden, 0, 1).reshape(3, 2 * hid, rows * half)
        other_hidden = other_core(hidden[:, hid:])

        def backward(weight, which):
            return jnp.einsum(
                "hrt,hzf->rztf",
                hidden[which].reshape(2 * hid, rows, half),
                weight.reshape(2 * hid, count_z, 2 * feats),
                preferred_element_type=F32,
            )

        terms = jnp.stack(
            [backward(down_w, 0), backward(gate_w, 1) + backward(up_w, 2)], 2
        ).astype(BF)
        terms = over_row(terms).astype(F32).sum(0).astype(BF)
        terms = over_z(terms).astype(F32).sum(0)
        low, high = terms[..., :feats], terms[..., feats:]
        mine = jnp.where(first, low, high)
        theirs = other_core(jnp.where(first, high, low))
        done = jnp.where(
            first, jnp.concatenate([mine, theirs], 1), jnp.concatenate([theirs, mine], 1)
        )
        done = jnp.swapaxes(done, 1, 2)
        v_prev = (v_out - (1.0 - momentum) * done[0]) / momentum
        dx_prev = dx_out + done[1]

        def gradient(which, source):
            def term(hid_part, in_part):
                return jnp.einsum(
                    "hrt,rztf->hzf",
                    hid_part.reshape(hid, rows, half),
                    in_part,
                    preferred_element_type=F32,
                )

            total = term(hidden[which, :hid], inputs[:, :, source]) + term(
                other_hidden[which], other_inputs[:, :, source]
            )
            return total.reshape(hid, count_z * 2 * feats)

        return (x_prev, v_prev, dx_prev, gradient(1, 0), gradient(2, 0), gradient(0, 1))

    return on_device


def solution(mesh):
    tokens = P(("depth", "col"), "row")
    weights = P(("col", "row"), "depth")
    return jax.shard_map(
        make(mesh.shape["depth"], mesh.shape["row"], mesh.shape["col"]),
        mesh=mesh,
        in_specs=(tokens,) * 4 + (weights,) * 3,
        out_specs=(tokens,) * 3 + (weights,) * 3,
        check_vma=False,
    )
```

```python
import jax
import jax.numpy as jnp
from jax import lax
from jax.sharding import PartitionSpec as P

momentum = 0.5
BF = jnp.bfloat16
F32 = jnp.float32


def copies(block, count):
    return jnp.broadcast_to(block[None], (count,) + block.shape)


def dot(left, right, left_dim, right_dim):
    return lax.dot_general(
        left, right, (((left_dim,), (right_dim,)), ((), ())), preferred_element_type=F32
    )


def nonlinear(gate, up_val, d_act):
    sig = jax.nn.sigmoid(gate)
    act = (gate * sig * up_val).astype(BF)
    d_gate = (d_act * up_val * sig * (1.0 + gate * (1.0 - sig))).astype(BF)
    d_up = (d_act * gate * sig).astype(BF)
    return jnp.stack([act, d_gate, d_up])


def make(depth, rows, cols):
    count_x, count_z = depth // 2, cols // 2
    x_groups = [[2 * x + h for x in range(count_x)] for h in range(2)]
    z_groups = [[2 * z + k for z in range(count_z)] for k in range(2)]
    swap_core = [(c, c ^ 1) for c in range(cols)]
    swap_half = [(d, d ^ 1) for d in range(depth)]

    def over_x(blocks):
        return lax.all_to_all(blocks, "depth", 0, 0, axis_index_groups=x_groups)

    def over_z(blocks):
        return lax.all_to_all(blocks, "col", 0, 0, axis_index_groups=z_groups)

    def over_row(blocks):
        return lax.all_to_all(blocks, "row", 0, 0)

    def other_core(block):
        return lax.ppermute(block, "col", swap_core)

    def other_half(block):
        return lax.ppermute(block, "depth", swap_half)

    def on_device(x_out, v_out, dx_out, dv_out, gate_weight, up_weight, down_weight):
        feats, toks = x_out.shape
        half = toks // 2
        hid = gate_weight.shape[0]
        part = 2 * hid // count_x
        tokens = rows * half
        wide = count_z * 2 * feats
        first = lax.axis_index("col") % 2 == 0

        def pick(one, two):
            return jnp.where(first, one, two)

        x_prev = x_out - v_out
        x_half = x_prev.astype(BF)
        df_half = ((1.0 - momentum) * (dx_out + dv_out)).astype(BF)
        both = jnp.stack([x_half.T, df_half.T]).reshape(2, 2, half, feats)
        mine = pick(both[:, 0], both[:, 1])
        theirs = other_core(pick(both[:, 1], both[:, 0]))
        block = pick(
            jnp.concatenate([mine, theirs], -1), jnp.concatenate([theirs, mine], -1)
        )
        block, gate_weight, up_weight, down_weight = lax.optimization_barrier(
            (block, gate_weight, up_weight, down_weight)
        )

        gate_w = jnp.concatenate([gate_weight, other_core(gate_weight)])
        up_w = jnp.concatenate([up_weight, other_core(up_weight)])
        down_w = jnp.concatenate([down_weight, other_core(down_weight)])

        along_z = jnp.swapaxes(over_z(copies(block, count_z)), 0, 1)
        inputs = over_row(copies(along_z, rows))

        def matrix(which):
            return jnp.swapaxes(inputs[:, which], 1, 2).reshape(tokens, wide)

        x_mat, df_mat = matrix(0), matrix(1)

        def hidden_part(weight, mat):
            return dot(weight, mat, 1, 1).astype(BF).reshape(count_x, 1, part, tokens)

        parts = jnp.concatenate(
            [hidden_part(gate_w, x_mat), hidden_part(up_w, x_mat), hidden_part(down_w, df_mat)], 1
        )
        sums = over_x(parts).astype(F32).sum(0)
        sums = sums + other_half(sums.astype(BF)).astype(F32)
        hidden = over_x(copies(nonlinear(sums[0], sums[1], sums[2]), count_x))
        act, d_gate, d_up = [hidden[:, i].reshape(2 * hid, tokens) for i in range(3)]

        y_part = dot(act, down_w, 0, 0)
        dx_part = dot(d_gate, gate_w, 0, 0) + dot(d_up, up_w, 0, 0)

        def blocks_of(total):
            blocks = total.astype(BF).reshape(rows, half, count_z, 2 * feats)
            return jnp.swapaxes(blocks, 1, 2)

        terms = jnp.stack([blocks_of(y_part), blocks_of(dx_part)], 2)
        terms = over_row(terms).astype(F32).sum(0).astype(BF)
        terms = over_z(terms).astype(F32).sum(0)
        low, high = terms[..., :feats], terms[..., feats:]
        theirs = other_core(pick(high, low))
        mine = pick(low, high)
        done = pick(jnp.concatenate([mine, theirs], 1), jnp.concatenate([theirs, mine], 1))
        v_prev = (v_out - (1.0 - momentum) * done[0].T) / momentum
        dx_prev = dx_out + done[1].T

        x_far, df_far = other_core(x_mat), other_core(df_mat)
        hidden_far = other_core(hidden[count_x // 2 :])

        def gradient(which, near, far):
            mine = hidden[: count_x // 2, which].reshape(hid, tokens)
            theirs = hidden_far[:, which].reshape(hid, tokens)
            return dot(mine, near, 1, 0) + dot(theirs, far, 1, 0)

        grad_down = gradient(0, df_mat, df_far)
        grad_gate = gradient(1, x_mat, x_far)
        grad_up = gradient(2, x_mat, x_far)
        return (x_prev, v_prev, dx_prev, grad_gate, grad_up, grad_down)

    return on_device


def solution(mesh):
    tokens = P(("depth", "col"), "row")
    weights = P(("col", "row"), "depth")
    return jax.shard_map(
        make(mesh.shape["depth"], mesh.shape["row"], mesh.shape["col"]),
        mesh=mesh,
        in_specs=(tokens,) * 4 + (weights,) * 3,
        out_specs=(tokens,) * 3 + (weights,) * 3,
        check_vma=False,
    )
```

```python
import jax
import jax.numpy as jnp
from jax import lax
from jax.experimental import pallas as pl
from jax.experimental.pallas import tpu as pltpu
from jax.sharding import PartitionSpec as P

momentum = 0.5
BF = jnp.bfloat16
F32 = jnp.float32


def copies(block, count):
    return jnp.broadcast_to(block[None], (count,) + block.shape)


def dot(left, right, left_dim, right_dim):
    return lax.dot_general(
        left, right, (((left_dim,), (right_dim,)), ((), ())), preferred_element_type=F32
    )


def nonlinear(gate, up_val, d_act):
    sig = jax.nn.sigmoid(gate)
    act = (gate * sig * up_val).astype(BF)
    d_gate = (d_act * up_val * sig * (1.0 + gate * (1.0 - sig))).astype(BF)
    d_up = (d_act * gate * sig).astype(BF)
    return jnp.stack([act, d_gate, d_up])


def sum_kernel(in_ref, out_ref):
    total = in_ref[0].astype(F32)
    for row in range(1, in_ref.shape[0]):
        total += in_ref[row].astype(F32)
    for piece in range(out_ref.shape[0]):
        out_ref[piece] = total[:, :, piece * 128 : (piece + 1) * 128].astype(BF)


def sum_rows(terms, lanes=256):
    rows, arrays, toks, wide = terms.shape
    return pl.pallas_call(
        sum_kernel,
        grid=(wide // lanes,),
        in_specs=[pl.BlockSpec((rows, arrays, toks, lanes), lambda i: (0, 0, 0, i))],
        out_specs=pl.BlockSpec((lanes // 128, arrays, toks, 128), lambda i: (i, 0, 0, 0)),
        out_shape=jax.ShapeDtypeStruct((wide // 128, arrays, toks, 128), BF),
        compiler_params=pltpu.CompilerParams(vmem_limit_bytes=32 * 1024 * 1024),
    )(terms)


def make(depth, rows, cols):
    count_x, count_z = depth // 2, cols // 2
    x_groups = [[2 * x + h for x in range(count_x)] for h in range(2)]
    z_groups = [[2 * z + k for z in range(count_z)] for k in range(2)]
    swap_core = [(c, c ^ 1) for c in range(cols)]
    swap_half = [(d, d ^ 1) for d in range(depth)]

    def over_x(blocks):
        return lax.all_to_all(blocks, "depth", 0, 0, axis_index_groups=x_groups)

    def over_z(blocks):
        return lax.all_to_all(blocks, "col", 0, 0, axis_index_groups=z_groups)

    def gather_z(block, place):
        span = count_z // 2
        pairs = [(c, (c + 2 * span) % cols) for c in range(cols)]
        groups = [
            [2 * (end * span + z) + k for z in range(span)] for end in range(2) for k in range(2)
        ]
        far = lax.ppermute(block, "col", pairs)
        low = place < span
        both = jnp.stack([jnp.where(low, block, far), jnp.where(low, far, block)])
        both = lax.all_to_all(copies(both, span), "col", 0, 0, axis_index_groups=groups)
        return jnp.swapaxes(both, 0, 1).reshape((count_z,) + block.shape)

    def over_row(blocks):
        return lax.all_to_all(blocks, "row", 0, 0)

    def other_core(block):
        return lax.ppermute(block, "col", swap_core)

    def other_half(block):
        return lax.ppermute(block, "depth", swap_half)

    def on_device(x_out, v_out, dx_out, dv_out, gate_weight, up_weight, down_weight):
        feats, toks = x_out.shape
        half = toks // 2
        hid = gate_weight.shape[0]
        part = 2 * hid // count_x
        tokens = rows * half
        wide = count_z * 2 * feats
        first = lax.axis_index("col") % 2 == 0

        def pick(one, two):
            return jnp.where(first, one, two)

        x_prev = x_out - v_out
        x_half = x_prev.astype(BF)
        df_half = ((1.0 - momentum) * (dx_out + dv_out)).astype(BF)
        both = jnp.stack([x_half.T, df_half.T]).reshape(2, 2, half, feats)
        mine = pick(both[:, 0], both[:, 1])
        theirs = other_core(pick(both[:, 1], both[:, 0]))
        block = pick(
            jnp.concatenate([mine, theirs], -1), jnp.concatenate([theirs, mine], -1)
        )
        block, gate_weight, up_weight, down_weight = lax.optimization_barrier(
            (block, gate_weight, up_weight, down_weight)
        )

        gate_w = jnp.concatenate([gate_weight, other_core(gate_weight)])
        up_w = jnp.concatenate([up_weight, other_core(up_weight)])
        down_w = jnp.concatenate([down_weight, other_core(down_weight)])

        along_z = jnp.swapaxes(gather_z(block, lax.axis_index("col") // 2), 0, 1)
        inputs = over_row(copies(along_z, rows))

        def matrix(which):
            return jnp.swapaxes(inputs[:, which], 1, 2).reshape(tokens, wide)

        x_mat, df_mat = matrix(0), matrix(1)

        def hidden_part(weight, mat):
            return dot(weight, mat, 1, 1).astype(BF).reshape(count_x, 1, part, tokens)

        parts = jnp.concatenate(
            [hidden_part(gate_w, x_mat), hidden_part(up_w, x_mat), hidden_part(down_w, df_mat)], 1
        )
        sums = over_x(parts).astype(F32).sum(0)
        sums = sums + other_half(sums.astype(BF)).astype(F32)
        hidden = over_x(copies(nonlinear(sums[0], sums[1], sums[2]), count_x))
        act, d_gate, d_up = [hidden[:, i].reshape(2 * hid, tokens) for i in range(3)]

        y_part = dot(act, down_w, 0, 0)
        dx_part = dot(d_gate, gate_w, 0, 0) + dot(d_up, up_w, 0, 0)

        def blocks_of(total):
            return total.astype(BF).reshape(rows, half, wide)

        terms = sum_rows(over_row(jnp.stack([blocks_of(y_part), blocks_of(dx_part)], 1)))
        terms = over_z(terms)
        x_far, df_far = other_core(x_mat), other_core(df_mat)
        hidden_far = other_core(hidden[count_x // 2 :])

        def gradient(which, near, far):
            mine = hidden[: count_x // 2, which].reshape(hid, tokens)
            theirs = hidden_far[:, which].reshape(hid, tokens)
            return dot(mine, near, 1, 0) + dot(theirs, far, 1, 0)

        grad_down = gradient(0, df_mat, df_far)
        grad_gate = gradient(1, x_mat, x_far)
        grad_up = gradient(2, x_mat, x_far)
        terms, grad_gate, grad_up, grad_down = lax.optimization_barrier(
            (terms, grad_gate, grad_up, grad_down)
        )
        terms = terms.astype(F32).sum(0)
        low, high = terms[..., :feats], terms[..., feats:]
        theirs = other_core(pick(high, low))
        mine = pick(low, high)
        done = pick(jnp.concatenate([mine, theirs], 1), jnp.concatenate([theirs, mine], 1))
        v_prev = (v_out - (1.0 - momentum) * done[0].T) / momentum
        dx_prev = dx_out + done[1].T

        return (x_prev, v_prev, dx_prev, grad_gate, grad_up, grad_down)

    return on_device


def solution(mesh):
    tokens = P(("depth", "col"), "row")
    weights = P(("col", "row"), "depth")
    return jax.shard_map(
        make(mesh.shape["depth"], mesh.shape["row"], mesh.shape["col"]),
        mesh=mesh,
        in_specs=(tokens,) * 4 + (weights,) * 3,
        out_specs=(tokens,) * 3 + (weights,) * 3,
        check_vma=False,
    )
```

```python
import jax
import jax.numpy as jnp
from jax import lax
from jax.experimental import pallas as pl
from jax.experimental.pallas import tpu as pltpu
from jax.sharding import PartitionSpec as P

momentum = 0.5
BF = jnp.bfloat16
F32 = jnp.float32
together = lax.optimization_barrier


def copies(block, count):
    return jnp.broadcast_to(block[None], (count,) + block.shape)


def dot(left, right, left_dim, right_dim):
    return lax.dot_general(
        left, right, (((left_dim,), (right_dim,)), ((), ())), preferred_element_type=F32
    )


def nonlinear(gate, up_val, d_act):
    sig = jax.nn.sigmoid(gate)
    act = (gate * sig * up_val).astype(BF)
    d_gate = (d_act * up_val * sig * (1.0 + gate * (1.0 - sig))).astype(BF)
    d_up = (d_act * gate * sig).astype(BF)
    return jnp.stack([act, d_gate, d_up])


def sum_kernel(in_ref, out_ref):
    total = in_ref[0].astype(F32)
    for row in range(1, in_ref.shape[0]):
        total += in_ref[row].astype(F32)
    for piece in range(out_ref.shape[0]):
        out_ref[piece] = total[:, :, piece * 128 : (piece + 1) * 128].astype(BF)


def sum_rows(terms, lanes=256):
    rows, arrays, toks, wide = terms.shape
    return pl.pallas_call(
        sum_kernel,
        grid=(wide // lanes,),
        in_specs=[pl.BlockSpec((rows, arrays, toks, lanes), lambda i: (0, 0, 0, i))],
        out_specs=pl.BlockSpec((lanes // 128, arrays, toks, 128), lambda i: (i, 0, 0, 0)),
        out_shape=jax.ShapeDtypeStruct((wide // 128, arrays, toks, 128), BF),
        compiler_params=pltpu.CompilerParams(vmem_limit_bytes=32 * 1024 * 1024),
    )(terms)


def make(depth, rows, cols):
    count_x, count_z = depth // 2, cols // 2
    x_groups = [[2 * x + h for x in range(count_x)] for h in range(2)]
    z_groups = [[2 * z + k for z in range(count_z)] for k in range(2)]
    swap_core = [(c, c ^ 1) for c in range(cols)]
    swap_half = [(d, d ^ 1) for d in range(depth)]

    def over_x(blocks):
        return lax.all_to_all(blocks, "depth", 0, 0, axis_index_groups=x_groups)

    def over_z(blocks):
        return lax.all_to_all(blocks, "col", 0, 0, axis_index_groups=z_groups)

    def across_z(block):
        span = count_z // 2
        return lax.ppermute(block, "col", [(c, (c + 2 * span) % cols) for c in range(cols)])

    def gather_half(block, far, place):
        span = count_z // 2
        groups = [
            [2 * (end * span + z) + k for z in range(span)] for end in range(2) for k in range(2)
        ]
        low = place < span
        both = jnp.stack([jnp.where(low, block, far), jnp.where(low, far, block)])
        both = lax.all_to_all(copies(both, span), "col", 0, 0, axis_index_groups=groups)
        return jnp.swapaxes(both, 0, 1).reshape((count_z,) + block.shape)

    def over_row(blocks):
        return lax.all_to_all(blocks, "row", 0, 0)

    def other_core(block):
        return lax.ppermute(block, "col", swap_core)

    def other_half(block):
        return lax.ppermute(block, "depth", swap_half)

    def on_device(x_out, v_out, dx_out, dv_out, gate_weight, up_weight, down_weight):
        feats, toks = x_out.shape
        half = toks // 2
        hid = gate_weight.shape[0]
        part = 2 * hid // count_x
        tokens = rows * half
        wide = count_z * 2 * feats
        first = lax.axis_index("col") % 2 == 0

        def pick(one, two):
            return jnp.where(first, one, two)

        x_prev = x_out - v_out
        x_half = x_prev.astype(BF)
        df_half = ((1.0 - momentum) * (dx_out + dv_out)).astype(BF)
        both = jnp.stack([x_half.T, df_half.T]).reshape(2, 2, half, feats)
        mine = pick(both[:, 0], both[:, 1])
        theirs = other_core(pick(both[:, 1], both[:, 0]))
        block = pick(
            jnp.concatenate([mine, theirs], -1), jnp.concatenate([theirs, mine], -1)
        )
        block, gate_weight, up_weight, down_weight = together(
            (block, gate_weight, up_weight, down_weight)
        )
        along_z = gather_half(block, across_z(block), lax.axis_index("col") // 2)
        weights = jnp.concatenate([gate_weight, up_weight, down_weight], 1)
        weights = jnp.concatenate([weights, other_core(weights)])
        along_z, weights = together((along_z, weights))
        gate_w, up_w, down_w = [weights[:, i * wide : (i + 1) * wide] for i in range(3)]
        along_z = along_z.transpose(1, 2, 0, 3).reshape(2, half, wide)
        inputs = over_row(copies(along_z, rows))

        x_mat, df_mat = [inputs[:, which].reshape(tokens, wide) for which in range(2)]

        def hidden_part(weight, mat):
            return dot(weight, mat, 1, 1).astype(BF).reshape(count_x, 1, part, tokens)

        parts = jnp.concatenate(
            [hidden_part(gate_w, x_mat), hidden_part(up_w, x_mat), hidden_part(down_w, df_mat)], 1
        )
        sums = over_x(parts).astype(F32).sum(0)
        sums = sums + other_half(sums.astype(BF)).astype(F32)
        hidden = over_x(copies(nonlinear(sums[0], sums[1], sums[2]), count_x))
        act, d_gate, d_up = [hidden[:, i].reshape(2 * hid, tokens) for i in range(3)]

        y_part = dot(act, down_w, 0, 0)
        dx_part = dot(d_gate, gate_w, 0, 0) + dot(d_up, up_w, 0, 0)

        def blocks_of(total):
            return total.astype(BF).reshape(rows, half, wide)

        terms = sum_rows(over_row(jnp.stack([blocks_of(y_part), blocks_of(dx_part)], 1)))
        terms, late, v_late, dx_late, x_mat, df_mat = together(
            (terms, hidden, v_out, dx_out, x_mat, df_mat)
        )
        terms = over_z(terms)
        x_far, df_far = other_core(x_mat), other_core(df_mat)
        hidden_far = other_core(late[count_x // 2 :])

        def gradient(which, near, far):
            mine = late[: count_x // 2, which].reshape(hid, tokens)
            theirs = hidden_far[:, which].reshape(hid, tokens)
            return dot(mine, near, 1, 0) + dot(theirs, far, 1, 0)

        grad_down = gradient(0, df_mat, df_far)
        grad_gate = gradient(1, x_mat, x_far)
        grad_up = gradient(2, x_mat, x_far)
        terms, grad_gate, grad_up, grad_down = together(
            (terms, grad_gate, grad_up, grad_down)
        )
        terms = terms.astype(F32).sum(0)
        low, high = terms[..., :feats], terms[..., feats:]
        theirs = other_core(pick(high, low))
        mine = pick(low, high)
        done = pick(jnp.concatenate([mine, theirs], 1), jnp.concatenate([theirs, mine], 1))
        v_prev = (v_late - (1.0 - momentum) * done[0].T) / momentum
        dx_prev = dx_late + done[1].T

        return (x_prev, v_prev, dx_prev, grad_gate, grad_up, grad_down)

    return on_device


def solution(mesh):
    tokens = P(("depth", "col"), "row")
    weights = P(("col", "row"), "depth")
    return jax.shard_map(
        make(mesh.shape["depth"], mesh.shape["row"], mesh.shape["col"]),
        mesh=mesh,
        in_specs=(tokens,) * 4 + (weights,) * 3,
        out_specs=(tokens,) * 3 + (weights,) * 3,
        check_vma=False,
    )
```

```python
import jax
import jax.numpy as jnp
from jax import lax
from jax.experimental import pallas as pl
from jax.experimental.pallas import tpu as pltpu
from jax.sharding import PartitionSpec as P

momentum = 0.5
BF = jnp.bfloat16
F32 = jnp.float32
together = lax.optimization_barrier


def copies(block, count):
    return jnp.broadcast_to(block[None], (count,) + block.shape)


def dot(left, right, left_dim, right_dim):
    return lax.dot_general(
        left, right, (((left_dim,), (right_dim,)), ((), ())), preferred_element_type=F32
    )


def nonlinear(gate, up_val, d_act):
    sig = jax.nn.sigmoid(gate)
    act = (gate * sig * up_val).astype(BF)
    d_gate = (d_act * up_val * sig * (1.0 + gate * (1.0 - sig))).astype(BF)
    d_up = (d_act * gate * sig).astype(BF)
    return jnp.stack([act, d_gate, d_up])


def sum_kernel(in_ref, out_ref):
    for piece in range(out_ref.shape[0]):
        lanes = slice(piece * 128, (piece + 1) * 128)
        total = in_ref[0, :, :, lanes].astype(F32)
        for row in range(1, in_ref.shape[0]):
            total += in_ref[row, :, :, lanes].astype(F32)
        out_ref[piece] = total.astype(BF)


def sum_rows(terms):
    rows, arrays, toks, wide = terms.shape
    return pl.pallas_call(
        sum_kernel,
        in_specs=[pl.BlockSpec(memory_space=pltpu.VMEM)],
        out_specs=pl.BlockSpec(memory_space=pltpu.VMEM),
        out_shape=jax.ShapeDtypeStruct((wide // 128, arrays, toks, 128), BF),
        compiler_params=pltpu.CompilerParams(vmem_limit_bytes=32 * 1024 * 1024),
    )(terms)


def make(depth, rows, cols):
    count_x, count_z = depth // 2, cols // 2
    x_groups = [[2 * x + h for x in range(count_x)] for h in range(2)]
    z_groups = [[2 * z + k for z in range(count_z)] for k in range(2)]
    swap_core = [(c, c ^ 1) for c in range(cols)]
    swap_half = [(d, d ^ 1) for d in range(depth)]

    def over_x(blocks):
        return lax.all_to_all(blocks, "depth", 0, 0, axis_index_groups=x_groups)

    def over_z(blocks):
        return lax.all_to_all(blocks, "col", 0, 0, axis_index_groups=z_groups)

    def across_z(block, flip):
        return lax.ppermute(block, "col", [(c, (c + count_z) % cols ^ flip) for c in range(cols)])

    def gather_half(block, far, place):
        span = count_z // 2
        groups = [
            [2 * (end * span + z) + k for z in range(span)] for end in range(2) for k in range(2)
        ]
        low = place < span
        both = jnp.stack([jnp.where(low, block, far), jnp.where(low, far, block)])
        both = lax.all_to_all(copies(both, span), "col", 0, 0, axis_index_groups=groups)
        return jnp.swapaxes(both, 0, 1).reshape((count_z,) + block.shape)

    def over_row(blocks):
        return lax.all_to_all(blocks, "row", 0, 0)

    def other_core(block):
        return lax.ppermute(block, "col", swap_core)

    def other_half(block):
        return lax.ppermute(block, "depth", swap_half)

    def on_device(x_out, v_out, dx_out, dv_out, gate_weight, up_weight, down_weight):
        feats, toks = x_out.shape
        half = toks // 2
        hid = gate_weight.shape[0]
        part = 2 * hid // count_x
        tokens = rows * half
        wide = count_z * 2 * feats
        first = lax.axis_index("col") % 2 == 0

        def pick(one, two):
            return jnp.where(first, one, two)

        x_prev = x_out - v_out
        x_half = x_prev.astype(BF)
        df_half = ((1.0 - momentum) * (dx_out + dv_out)).astype(BF)
        both = jnp.stack([x_half.T, df_half.T]).reshape(2, 2, half, feats)
        mine, theirs = pick(both[:, 0], both[:, 1]), pick(both[:, 1], both[:, 0])
        mine, theirs, gate_weight, up_weight, down_weight = together(
            (mine, theirs, gate_weight, up_weight, down_weight)
        )

        def chip_block(own, other):
            return pick(
                jnp.concatenate([own, other], -1), jnp.concatenate([other, own], -1)
            )

        block = chip_block(mine, other_core(theirs))
        far = chip_block(across_z(mine, 0), across_z(theirs, 1))

        along_z = gather_half(block, far, lax.axis_index("col") // 2)
        weights = jnp.concatenate([gate_weight, up_weight, down_weight], 1)
        weights = jnp.concatenate([weights, other_core(weights)])
        along_z, weights = together((along_z, weights))
        gate_w, up_w, down_w = [weights[:, i * wide : (i + 1) * wide] for i in range(3)]
        along_z = along_z.transpose(1, 2, 0, 3).reshape(2, half, wide)
        inputs = over_row(copies(along_z, rows))

        x_mat, df_mat = [inputs[:, which].reshape(tokens, wide) for which in range(2)]

        def hidden_part(weight, mat):
            return dot(weight, mat, 1, 1).astype(BF).reshape(count_x, 1, part, tokens)

        parts = jnp.concatenate(
            [hidden_part(gate_w, x_mat), hidden_part(up_w, x_mat), hidden_part(down_w, df_mat)], 1
        )
        sums = over_x(parts).astype(F32).sum(0)
        sums = sums + other_half(sums.astype(BF)).astype(F32)
        hidden = over_x(copies(nonlinear(sums[0], sums[1], sums[2]), count_x))
        act, d_gate, d_up = [hidden[:, i].reshape(2 * hid, tokens) for i in range(3)]

        y_part = dot(act, down_w, 0, 0)
        dx_part = dot(d_gate, gate_w, 0, 0) + dot(d_up, up_w, 0, 0)

        def blocks_of(total):
            return total.astype(BF).reshape(rows, half, wide)

        terms = sum_rows(over_row(jnp.stack([blocks_of(y_part), blocks_of(dx_part)], 1)))
        terms, late, v_late, dx_late, x_mat, df_mat = together(
            (terms, hidden, v_out, dx_out, x_mat, df_mat)
        )
        terms = over_z(terms)
        x_far, df_far = other_core(x_mat), other_core(df_mat)
        hidden_far = other_core(late[count_x // 2 :])

        def gradient(which, near, far):
            mine = late[: count_x // 2, which].reshape(hid, tokens)
            theirs = hidden_far[:, which].reshape(hid, tokens)
            return dot(mine, near, 1, 0) + dot(theirs, far, 1, 0)

        grad_down = gradient(0, df_mat, df_far)
        grad_gate = gradient(1, x_mat, x_far)
        grad_up = gradient(2, x_mat, x_far)
        terms, grad_gate, grad_up, grad_down = together(
            (terms, grad_gate, grad_up, grad_down)
        )
        terms = terms.astype(F32).sum(0)
        low, high = terms[..., :feats], terms[..., feats:]
        theirs = other_core(pick(high, low))
        mine = pick(low, high)
        done = pick(jnp.concatenate([mine, theirs], 1), jnp.concatenate([theirs, mine], 1))
        v_prev = (v_late - (1.0 - momentum) * done[0].T) / momentum
        dx_prev = dx_late + done[1].T

        return (x_prev, v_prev, dx_prev, grad_gate, grad_up, grad_down)

    return on_device


def solution(mesh):
    tokens = P(("depth", "col"), "row")
    weights = P(("col", "row"), "depth")
    return jax.shard_map(
        make(mesh.shape["depth"], mesh.shape["row"], mesh.shape["col"]),
        mesh=mesh,
        in_specs=(tokens,) * 4 + (weights,) * 3,
        out_specs=(tokens,) * 3 + (weights,) * 3,
        check_vma=False,
    )
```

```python
import jax
import jax.numpy as jnp
from jax import lax
from jax.experimental import pallas as pl
from jax.experimental.pallas import tpu as pltpu
from jax.sharding import PartitionSpec as P

momentum = 0.5
BF = jnp.bfloat16
F32 = jnp.float32
together = lax.optimization_barrier


def copies(block, count):
    return jnp.broadcast_to(block[None], (count,) + block.shape)


def dot(left, right, left_dim, right_dim):
    return lax.dot_general(
        left, right, (((left_dim,), (right_dim,)), ((), ())), preferred_element_type=F32
    )


def nonlinear(gate, up_val, d_act):
    sig = jax.nn.sigmoid(gate)
    act = (gate * sig * up_val).astype(BF)
    d_gate = (d_act * up_val * sig * (1.0 + gate * (1.0 - sig))).astype(BF)
    d_up = (d_act * gate * sig).astype(BF)
    return jnp.stack([act, d_gate, d_up])


def sum_kernel(in_ref, out_ref):
    for piece in range(out_ref.shape[0]):
        lanes = slice(piece * 128, (piece + 1) * 128)
        total = in_ref[0, :, :, lanes].astype(F32)
        for row in range(1, in_ref.shape[0]):
            total += in_ref[row, :, :, lanes].astype(F32)
        out_ref[piece] = total.astype(BF)


def sum_rows(terms):
    rows, arrays, toks, wide = terms.shape
    return pl.pallas_call(
        sum_kernel,
        in_specs=[pl.BlockSpec(memory_space=pltpu.VMEM)],
        out_specs=pl.BlockSpec(memory_space=pltpu.VMEM),
        out_shape=jax.ShapeDtypeStruct((wide // 128, arrays, toks, 128), BF),
        compiler_params=pltpu.CompilerParams(vmem_limit_bytes=32 * 1024 * 1024),
    )(terms)


def make(depth, rows, cols):
    count_x, count_z = depth // 2, cols // 2
    x_groups = [[2 * x + h for x in range(count_x)] for h in range(2)]
    z_groups = [[2 * z + k for z in range(count_z)] for k in range(2)]
    swap_core = [(c, c ^ 1) for c in range(cols)]
    swap_half = [(d, d ^ 1) for d in range(depth)]

    def over_x(blocks):
        return lax.all_to_all(blocks, "depth", 0, 0, axis_index_groups=x_groups)

    def over_z(blocks):
        return lax.all_to_all(blocks, "col", 0, 0, axis_index_groups=z_groups)

    def across_z(block, flip):
        return lax.ppermute(block, "col", [(c, (c + count_z) % cols ^ flip) for c in range(cols)])

    def gather_half(block, far, place):
        span = count_z // 2
        groups = [
            [2 * (end * span + z) + k for z in range(span)] for end in range(2) for k in range(2)
        ]
        low = place < span
        both = jnp.stack([jnp.where(low, block, far), jnp.where(low, far, block)])
        both = lax.all_to_all(copies(both, span), "col", 0, 0, axis_index_groups=groups)
        return jnp.swapaxes(both, 0, 1).reshape((count_z,) + block.shape)

    def over_row(blocks):
        return lax.all_to_all(blocks, "row", 0, 0)

    def other_core(block):
        return lax.ppermute(block, "col", swap_core)

    def other_half(block):
        return lax.ppermute(block, "depth", swap_half)

    def on_device(x_out, v_out, dx_out, dv_out, gate_weight, up_weight, down_weight):
        feats, toks = x_out.shape
        half = toks // 2
        hid = gate_weight.shape[0]
        part = 2 * hid // count_x
        tokens = rows * half
        wide = count_z * 2 * feats
        first = lax.axis_index("col") % 2 == 0

        def pick(one, two):
            return jnp.where(first, one, two)

        x_half = (x_out - v_out).astype(BF)
        df_half = ((1.0 - momentum) * (dx_out + dv_out)).astype(BF)
        both = jnp.stack([x_half.T, df_half.T]).reshape(2, 2, half, feats)
        mine, theirs = pick(both[:, 0], both[:, 1]), pick(both[:, 1], both[:, 0])
        mine, theirs, gate_weight, up_weight, down_weight = together(
            (mine, theirs, gate_weight, up_weight, down_weight)
        )

        def chip_block(own, other):
            return pick(
                jnp.concatenate([own, other], -1), jnp.concatenate([other, own], -1)
            )

        block = chip_block(mine, other_core(theirs))
        far = chip_block(across_z(mine, 0), across_z(theirs, 1))

        along_z = gather_half(block, far, lax.axis_index("col") // 2)
        weights = jnp.concatenate([gate_weight, up_weight, down_weight], 1)
        weights = jnp.concatenate([weights, other_core(weights)])
        along_z, weights = together((along_z, weights))
        gate_w, up_w, down_w = [weights[:, i * wide : (i + 1) * wide] for i in range(3)]
        along_z = along_z.transpose(1, 2, 0, 3).reshape(2, half, wide)
        inputs = over_row(copies(along_z, rows))

        x_mat, df_mat = [inputs[:, which].reshape(tokens, wide) for which in range(2)]

        def hidden_part(weight, mat):
            return dot(weight, mat, 1, 1).astype(BF).reshape(count_x, 1, part, tokens)

        parts = jnp.concatenate(
            [hidden_part(gate_w, x_mat), hidden_part(up_w, x_mat), hidden_part(down_w, df_mat)], 1
        )
        sums = over_x(parts).astype(F32).sum(0)
        sums = sums + other_half(sums.astype(BF)).astype(F32)
        hidden = lax.all_gather(
            nonlinear(sums[0], sums[1], sums[2]), "depth", axis_index_groups=x_groups
        )
        act, d_gate, d_up = [hidden[:, i].reshape(2 * hid, tokens) for i in range(3)]

        y_part = dot(act, down_w, 0, 0)
        dx_part = dot(d_gate, gate_w, 0, 0) + dot(d_up, up_w, 0, 0)

        def blocks_of(total):
            return total.astype(BF).reshape(rows, half, wide)

        terms = sum_rows(over_row(jnp.stack([blocks_of(y_part), blocks_of(dx_part)], 1)))
        terms, late, x_late, v_late, dx_late, x_mat, df_mat = together(
            (terms, hidden, x_out, v_out, dx_out, x_mat, df_mat)
        )
        x_prev = x_late - v_late
        terms = over_z(terms)
        x_far, df_far = other_core(x_mat), other_core(df_mat)
        hidden_far = other_core(late[count_x // 2 :])

        def gradient(which, near, far):
            mine = late[: count_x // 2, which].reshape(hid, tokens)
            theirs = hidden_far[:, which].reshape(hid, tokens)
            return dot(mine, near, 1, 0) + dot(theirs, far, 1, 0)

        grad_down = gradient(0, df_mat, df_far)
        grad_gate = gradient(1, x_mat, x_far)
        grad_up = gradient(2, x_mat, x_far)
        terms, x_prev, grad_gate, grad_up, grad_down = together(
            (terms, x_prev, grad_gate, grad_up, grad_down)
        )
        terms = jnp.swapaxes(terms.astype(F32).sum(0), 1, 2)
        low, high = terms[:, :feats], terms[:, feats:]
        theirs = other_core(pick(high, low))
        mine = pick(low, high)
        done = pick(jnp.concatenate([mine, theirs], 2), jnp.concatenate([theirs, mine], 2))
        v_prev = (v_late - (1.0 - momentum) * done[0]) / momentum
        dx_prev = dx_late + done[1]
        return (x_prev, v_prev, dx_prev, grad_gate, grad_up, grad_down)

    return on_device


def solution(mesh):
    tokens = P(("depth", "col"), "row")
    weights = P(("col", "row"), "depth")
    return jax.shard_map(
        make(mesh.shape["depth"], mesh.shape["row"], mesh.shape["col"]),
        mesh=mesh,
        in_specs=(tokens,) * 4 + (weights,) * 3,
        out_specs=(tokens,) * 3 + (weights,) * 3,
        check_vma=False,
    )
```

```python
import jax
import jax.numpy as jnp
from jax import lax
from jax.experimental import pallas as pl
from jax.experimental.pallas import tpu as pltpu
from jax.sharding import PartitionSpec as P

momentum = 0.5
BF = jnp.bfloat16
F32 = jnp.float32
together = lax.optimization_barrier


def copies(block, count):
    return jnp.broadcast_to(block[None], (count,) + block.shape)


def dot(left, right, left_dim, right_dim):
    return lax.dot_general(
        left, right, (((left_dim,), (right_dim,)), ((), ())), preferred_element_type=F32
    )


def nonlinear(gate, up_val, d_act):
    sig = jax.nn.sigmoid(gate)
    act = (gate * sig * up_val).astype(BF)
    d_gate = (d_act * up_val * sig * (1.0 + gate * (1.0 - sig))).astype(BF)
    d_up = (d_act * gate * sig).astype(BF)
    return jnp.stack([act, d_gate, d_up])


def sum_kernel(in_ref, out_ref):
    for piece in range(out_ref.shape[0]):
        lanes = slice(piece * 128, (piece + 1) * 128)
        total = in_ref[0, :, :, lanes].astype(F32)
        for row in range(1, in_ref.shape[0]):
            total += in_ref[row, :, :, lanes].astype(F32)
        out_ref[piece] = total.astype(BF)


def sum_rows(terms):
    rows, arrays, toks, wide = terms.shape
    return pl.pallas_call(
        sum_kernel,
        in_specs=[pl.BlockSpec(memory_space=pltpu.VMEM)],
        out_specs=pl.BlockSpec(memory_space=pltpu.VMEM),
        out_shape=jax.ShapeDtypeStruct((wide // 128, arrays, toks, 128), BF),
        compiler_params=pltpu.CompilerParams(vmem_limit_bytes=32 * 1024 * 1024),
    )(terms)


def make(depth, rows, cols):
    count_x, count_z = depth // 2, cols // 2
    x_groups = [[2 * x + h for x in range(count_x)] for h in range(2)]
    z_groups = [[2 * z + k for z in range(count_z)] for k in range(2)]
    swap_core = [(c, c ^ 1) for c in range(cols)]
    swap_half = [(d, d ^ 1) for d in range(depth)]

    def over_x(blocks):
        return lax.all_to_all(blocks, "depth", 0, 0, axis_index_groups=x_groups)

    def over_z(blocks):
        return lax.all_to_all(blocks, "col", 0, 0, axis_index_groups=z_groups)

    def across_z(block, flip):
        return lax.ppermute(block, "col", [(c, (c + count_z) % cols ^ flip) for c in range(cols)])

    def gather_half(block, far, place):
        span = count_z // 2
        groups = [
            [2 * (end * span + z) + k for z in range(span)] for end in range(2) for k in range(2)
        ]
        low = place < span
        both = jnp.stack([jnp.where(low, block, far), jnp.where(low, far, block)])
        both = lax.all_to_all(copies(both, span), "col", 0, 0, axis_index_groups=groups)
        return jnp.swapaxes(both, 0, 1).reshape((count_z,) + block.shape)

    def over_row(blocks):
        return lax.all_to_all(blocks, "row", 0, 0)

    def other_core(block):
        return lax.ppermute(block, "col", swap_core)

    def other_half(block):
        return lax.ppermute(block, "depth", swap_half)

    def on_device(x_out, v_out, dx_out, dv_out, gate_weight, up_weight, down_weight):
        feats, toks = x_out.shape
        half = toks // 2
        hid = gate_weight.shape[0]
        part = 2 * hid // count_x
        tokens = rows * half
        wide = count_z * 2 * feats
        first = lax.axis_index("col") % 2 == 0

        def pick(one, two):
            return jnp.where(first, one, two)

        x_half = (x_out - v_out).astype(BF)
        df_half = ((1.0 - momentum) * (dx_out + dv_out)).astype(BF)
        both = jnp.stack([x_half.T, df_half.T]).reshape(2, 2, half, feats)
        mine, theirs = pick(both[:, 0], both[:, 1]), pick(both[:, 1], both[:, 0])
        mine, theirs, gate_weight, up_weight, down_weight = together(
            (mine, theirs, gate_weight, up_weight, down_weight)
        )

        def chip_block(own, other):
            return pick(
                jnp.concatenate([own, other], -1), jnp.concatenate([other, own], -1)
            )

        block = chip_block(mine, other_core(theirs))
        far = chip_block(across_z(mine, 0), across_z(theirs, 1))

        along_z = gather_half(block, far, lax.axis_index("col") // 2)
        weights = jnp.concatenate([gate_weight, up_weight, down_weight], 1)
        weights = jnp.concatenate([weights, other_core(weights)])
        along_z, weights = together((along_z, weights))
        gate_w, up_w, down_w = [weights[:, i * wide : (i + 1) * wide] for i in range(3)]
        along_z = along_z.transpose(1, 2, 0, 3).reshape(2, half, wide)
        inputs = over_row(copies(along_z, rows))

        x_mat, df_mat = [inputs[:, which].reshape(tokens, wide) for which in range(2)]

        def hidden_part(weight, mat):
            return dot(weight, mat, 1, 1).astype(BF).reshape(count_x, 1, part, tokens)

        parts = jnp.concatenate(
            [hidden_part(gate_w, x_mat), hidden_part(up_w, x_mat), hidden_part(down_w, df_mat)], 1
        )
        sums = over_x(parts).astype(F32).sum(0)
        sums = sums + other_half(sums.astype(BF)).astype(F32)
        hidden = lax.all_gather(
            nonlinear(sums[0], sums[1], sums[2]), "depth", axis_index_groups=x_groups
        )
        act, d_gate, d_up = [hidden[:, i].reshape(2 * hid, tokens) for i in range(3)]

        y_part = dot(act, down_w, 0, 0)
        dx_part = dot(d_gate, gate_w, 0, 0) + dot(d_up, up_w, 0, 0)

        def blocks_of(total):
            return total.astype(BF).reshape(rows, half, wide)

        terms = sum_rows(over_row(jnp.stack([blocks_of(y_part), blocks_of(dx_part)], 1)))
        terms, late, x_late, v_late, dx_late, x_mat, df_mat = together(
            (terms, hidden, x_out, v_out, dx_out, x_mat, df_mat)
        )
        x_prev = x_late - v_late
        terms = over_z(terms)
        x_far, df_far = other_core(x_mat), other_core(df_mat)
        hidden_far = other_core(late[count_x // 2 :])

        def gradient(which, near, far):
            mine = late[: count_x // 2, which].reshape(hid, tokens)
            theirs = hidden_far[:, which].reshape(hid, tokens)
            return dot(mine, near, 1, 0) + dot(theirs, far, 1, 0)

        grad_down = gradient(0, df_mat, df_far)
        grad_gate = gradient(1, x_mat, x_far)
        grad_up = gradient(2, x_mat, x_far)
        terms, x_prev, grad_gate, grad_up = together((terms, x_prev, grad_gate, grad_up))
        terms = jnp.swapaxes(terms.astype(F32).sum(0), 1, 2)
        low, high = terms[:, :feats], terms[:, feats:]
        theirs = other_core(pick(high, low))
        mine = pick(low, high)
        done = pick(jnp.concatenate([mine, theirs], 2), jnp.concatenate([theirs, mine], 2))
        v_prev = (v_late - (1.0 - momentum) * done[0]) / momentum
        dx_prev = dx_late + done[1]
        return (x_prev, v_prev, dx_prev, grad_gate, grad_up, grad_down)

    return on_device


def solution(mesh):
    tokens = P(("depth", "col"), "row")
    weights = P(("col", "row"), "depth")
    return jax.shard_map(
        make(mesh.shape["depth"], mesh.shape["row"], mesh.shape["col"]),
        mesh=mesh,
        in_specs=(tokens,) * 4 + (weights,) * 3,
        out_specs=(tokens,) * 3 + (weights,) * 3,
        check_vma=False,
    )
```
